32 devices in a mesh: row: 4 (over y, core), col: 8 (over z, x).
Axes of the slice: x: 2, y: 2, z: 4, core: 2. Of those that a mesh axis runs over, the one named last changes fastest.
Arguments:
- tokens: bfloat16 [256, 6144], P('col', 'row'), may hold values from -6 to 6
- target: bfloat16 [256, 6144], P('col', 'row'), may hold values from -6 to 6
- w_in: bfloat16 [6144, 24576], P('row', 'col'), may hold values from -0.078125 to 0.078125
- w_out: bfloat16 [6144, 24576], P('row', 'col'), may hold values from -0.0390625 to 0.0390625
- gains: float32 [2], replicated, may hold values from 2 to 6
- u_start: float32 [2, 6144], P(None, 'row'), may hold values from -6 to 6
Outputs:
- grad_tokens: bfloat16 [256, 6144], P('col', 'row')
- grad_in: bfloat16 [6144, 24576], P('row', 'col')
- grad_out: bfloat16 [6144, 24576], P('row', 'col')
- u_next: float32 [2, 6144], P(None, 'row')
The draws below stay inside these ranges and needn't reach their ends.
All inputs are finite; a program needn't handle non-finite values.
Results may differ from the reference program's by a relative error of at most 0.006.
Values may be sent and summed in bfloat16 or wider, within the bound.
A program may use at most 256 MiB of HBM per device.

```python
import math
import jax
import jax.numpy as jnp
from jax import lax

D = 6144
F = 24576
POWER = 2
TOKENS = 256


def shard_levels(key, extent, cuts, smallest, high):
    def one(axis_at, blocks):
        steps = jax.random.uniform(jax.random.fold_in(jax.random.fold_in(key, 6), axis_at), (blocks,), jnp.float32, smallest / len(cuts), high / len(cuts))
        return jnp.repeat(jnp.exp(steps), extent[axis_at] // blocks).reshape((-1,) + (1,) * (len(extent) - axis_at - 1))

    gain = one(*cuts[0])
    for cut in cuts[1:]:
        gain = gain * one(*cut)
    return gain


def scatter_about(key, shape, deviation, limit, shards=(), dtype=jnp.bfloat16):
    result = jax.random.normal(key, shape, jnp.float32) * deviation
    if len(shards) > 0:
        result = shard_levels(key, shape, shards, -0.22, 0.18) * result
    return jnp.clip(result, min=-limit, max=limit).astype(dtype)


def setup_inputs(seed: int = 0) -> dict:
    splits = jax.random.split(jax.random.key(seed), 7)
    tokens = scatter_about(splits[0], (TOKENS, D), 1.0, 6.0, ((0, 8), (1, 4)))
    target = scatter_about(splits[1], (TOKENS, D), 1.0, 6.0, ((0, 8), (1, 4)))
    w_in = scatter_about(splits[2], (D, F), D ** -0.5, 0.078125, ((0, 4), (1, 8)))
    w_out = scatter_about(splits[3], (D, F), F ** -0.5, 0.0390625, ((0, 4), (1, 8)))
    gains = jnp.clip(jnp.exp(jax.random.uniform(splits[4], (2,), jnp.float32, math.log(2.0), math.log(6.0))), 2.0, 6.0)
    u_start = scatter_about(splits[5], (2, D), 1.0, 6.0, ((1, 4),), jnp.float32)
    return {"tokens": tokens, "target": target, "w_in": w_in, "w_out": w_out, "gains": gains, "u_start": u_start}


EPSILON = 1e-06
ROOT_HALF = 0.7071067811865476
INV_ROOT_TWO_PI = 0.3989422804014327

def gelu_parts(values):
    normal_cdf = 0.5 * (1.0 + jax.scipy.special.erf(values * ROOT_HALF))
    active = values * normal_cdf
    slopes = normal_cdf + values * jnp.exp(-0.5 * values * values) * INV_ROOT_TWO_PI
    return (active, slopes)

def power_steps(weight, start):
    wide = weight.astype(jnp.float32)
    current = start
    for iteration in range(POWER):
        partial_value = jnp.dot(current, wide, precision=lax.Precision.HIGHEST)
        right_unit = partial_value / jnp.sqrt(jnp.sum(partial_value * partial_value) + EPSILON)
        left_vec = jnp.dot(wide, right_unit, precision=lax.Precision.HIGHEST)
        sigma = jnp.sqrt(jnp.sum(left_vec * left_vec) + EPSILON)
        current = left_vec / sigma
    return (current, right_unit, sigma)

def reference(tokens, target, w_in, w_out, gains, u_start):
    left_in, right_in, sigma_in = power_steps(w_in, u_start[0])
    left_out, right_out, sigma_out = power_steps(w_out, u_start[1])
    scale_in = gains[0] / sigma_in
    scale_out = gains[1] / sigma_out
    hidden = scale_in * jnp.dot(tokens, w_in, preferred_element_type=jnp.float32)
    active, slopes = gelu_parts(hidden)
    active = active.astype(jnp.bfloat16)
    output = scale_out * jnp.dot(active, w_out.T, preferred_element_type=jnp.float32)
    grad_output = ((output - target.astype(jnp.float32)) * (1.0 / jnp.sqrt(jnp.float32(TOKENS)))).astype(jnp.bfloat16)
    grad_active = scale_out * jnp.dot(grad_output, w_out, preferred_element_type=jnp.float32)
    grad_hidden = (grad_active * slopes).astype(jnp.bfloat16)
    block_in = jnp.dot(tokens.T, grad_hidden, preferred_element_type=jnp.float32)
    block_out = jnp.dot(grad_output.T, active, preferred_element_type=jnp.float32)
    trace_in = jnp.sum(block_in * w_in.astype(jnp.float32))
    trace_out = jnp.sum(block_out * w_out.astype(jnp.float32))
    grad_in = scale_in * block_in - scale_in * trace_in / sigma_in * (left_in[:, None] * right_in[None, :])
    grad_out = scale_out * block_out - scale_out * trace_out / sigma_out * (left_out[:, None] * right_out[None, :])
    grad_tokens = scale_in * jnp.dot(grad_hidden, w_in.T, preferred_element_type=jnp.float32)
    return (grad_tokens.astype(jnp.bfloat16), grad_in.astype(jnp.bfloat16), grad_out.astype(jnp.bfloat16), jnp.stack([left_in, left_out]))
```

```python
import functools

import jax
import jax.numpy as jnp
from jax import lax
from jax.experimental import pallas as pl
from jax.experimental.pallas import tpu as pltpu
from jax.sharding import PartitionSpec as P

POWER = 2
EPSILON = 1e-06
ROOT_HALF = 0.7071067811865476
INV_ROOT_TWO_PI = 0.3989422804014327
BF16 = jnp.bfloat16
F32 = jnp.float32
MESH = pl.DeviceIdType.MESH
LANES = 128


def tile_of(n):
    return 512 if n % 512 == 0 else 256


def pieces(vec):
    high = vec.astype(BF16).astype(F32)
    rest = vec - high
    mid = rest.astype(BF16).astype(F32)
    low = rest - mid
    row = lax.broadcasted_iota(jnp.int32, (16, vec.shape[1]), 0)
    stacked = jnp.where(row == 0, high, jnp.where(row == 1, mid, jnp.where(row == 2, low, 0.0)))
    return stacked.astype(BF16)


def body(
    rows_n, cols_n,
    tokens, target, gains, u_start, w_in_hbm, w_out_hbm,
    tok_all, act_all, g_all, gh_all, u_next, v_units, coeffs, grad_tokens,
    w_in, w_out, part, slopes, hid, own, s1, r1, s2, r2, outp, so, ro, pieces_l, pieces_r,
    uvec, left, right, p_buf, q_buf, n_buf, tr_buf, tc_buf,
    w_sem, out_sem,
    tok_s, tok_r, p_s, p_r, q_s, q_r, n_s, n_r, tr_s, tr_r, tc_s, tc_r,
    s1_s, s1_r, s2_s, s2_r, ag_s, ag_r, fw_s, fw_r, ro_s, ro_r, g_s, g_r,
):
    del out_sem
    row, col = lax.axis_index("row"), lax.axis_index("col")
    ys = rows_n // 2
    y, core = row // 2, row % 2
    mate = y * 2 + (1 - core)
    depth, width = w_in.shape
    total = tok_all.shape[0]
    block = total // cols_n
    chunk = total // rows_n

    loads = [
        pltpu.make_async_copy(w_in_hbm, w_in, w_sem.at[0]),
        pltpu.make_async_copy(w_out_hbm, w_out, w_sem.at[1]),
    ]
    for load in loads:
        load.start()

    barrier = pltpu.get_barrier_semaphore()
    for i in range(1, rows_n):
        pl.semaphore_signal(
            barrier, inc=1, device_id=((row + i) % rows_n, col), device_id_type=MESH
        )
    for i in range(1, cols_n):
        pl.semaphore_signal(
            barrier, inc=1, device_id=(row, (col + i) % cols_n), device_id_type=MESH
        )
    pl.semaphore_wait(barrier, rows_n + cols_n - 2)

    def remote(src, dst, send, recv, dev):
        return pltpu.make_async_remote_copy(
            src_ref=src, dst_ref=dst, send_sem=send, recv_sem=recv, device_id=dev,
            device_id_type=MESH,
        )

    def row_send(buf, send, recv):
        copies = []
        for i in range(1, rows_n):
            c = remote(buf.at[row], buf.at[row], send.at[i], recv.at[i],
                       ((row + i) % rows_n, col))
            c.start()
            copies.append(c)
        return copies

    def col_send(buf, send, recv):
        copies = []
        for i in range(1, cols_n):
            c = remote(buf.at[col], buf.at[col], send.at[i], recv.at[i],
                       (row, (col + i) % cols_n))
            c.start()
            copies.append(c)
        return copies

    def wait_all(copies):
        for c in copies:
            c.wait()

    def slot_sum(buf, n):
        acc = buf[0]
        for j in range(1, n):
            acc = acc + buf[j]
        return acc

    my_rows = pl.ds(pl.multiple_of(col * block, block), block)
    tok_all[my_rows, :] = tokens[...]
    tok_copies = []
    for i in range(1, cols_n):
        c = remote(tokens, tok_all.at[my_rows, :], tok_s.at[i], tok_r.at[i],
                   (row, (col + i) % cols_n))
        c.start()
        tok_copies.append(c)

    weights = (w_in, w_out)

    def times_left(k, vec):
        pieces_l[...] = pieces(vec)
        t = tile_of(width)

        def step(i, _):
            cs = pl.ds(pl.multiple_of(i * t, t), t)
            out = jnp.dot(pieces_l[...], weights[k][:, cs], preferred_element_type=F32)
            left[k : k + 1, cs] = jnp.sum(out, axis=0, keepdims=True)
            return 0

        lax.fori_loop(0, width // t, step, 0)

    def times_right(k, vec):
        pieces_r[...] = pieces(vec)
        t = 256

        def step(i, _):
            rs = pl.ds(pl.multiple_of(i * t, t), t)
            out = lax.dot_general(
                pieces_r[...], weights[k][rs, :], (((1,), (1,)), ((), ())),
                preferred_element_type=F32,
            )
            right[k : k + 1, rs] = jnp.sum(out, axis=0, keepdims=True)
            return 0

        lax.fori_loop(0, depth // t, step, 0)

    def matmul_nn(a, w):
        t = tile_of(width)

        def step(i, _):
            cs = pl.ds(pl.multiple_of(i * t, t), t)
            part[:, cs] = jnp.dot(a[...], w[:, cs], preferred_element_type=F32)
            return 0

        lax.fori_loop(0, width // t, step, 0)

    def matmul_nt(a, w):
        t = 256

        def step(i, _):
            cs = pl.ds(pl.multiple_of(i * t, t), t)
            outp[:, cs] = lax.dot_general(
                a[...], w[cs, :], (((1,), (1,)), ((), ())), preferred_element_type=F32
            )
            return 0

        lax.fori_loop(0, depth // t, step, 0)

    def rows_of(yy, cc):
        return pl.ds(pl.multiple_of((yy * 2 + cc) * chunk, chunk), chunk)

    def reduce_first(e):
        copies = []
        for yy in range(ys):
            s1[e, yy] = part[rows_of(yy, 1 - core), :].astype(BF16)
            c = remote(s1.at[e, yy], r1.at[e, yy], s1_s.at[e, yy], s1_r.at[e, yy], (mate, col))
            c.start()
            copies.append(c)
        return copies

    def reduce_second(e, first):
        wait_all(first)
        copies = []
        for i in range(1, ys):
            other = (y + i) % ys
            s2[e, i] = (part[rows_of(other, core), :] + r1[e, other].astype(F32)).astype(BF16)
            c = remote(s2.at[e, i], r2.at[e, i], s2_s.at[e, i], s2_r.at[e, i],
                       (other * 2 + core, col))
            c.start()
            copies.append(c)
        own[...] = part[rows_of(y, core), :] + r1[e, y].astype(F32)
        return copies

    def reduce_last(e, copies):
        wait_all(copies)
        acc = own[...]
        for i in range(1, ys):
            acc = acc + r2[e, i].astype(F32)
        return acc

    def gather_rows(e, buf):
        mine = rows_of(y, core)
        copies = []
        for i in range(1, ys):
            c = remote(buf.at[mine, :], buf.at[mine, :], ag_s.at[e, i], ag_r.at[e, i],
                       (((y + i) % ys) * 2 + core, col))
            c.start()
            copies.append(c)
        c = remote(buf.at[mine, :], buf.at[mine, :], fw_s.at[e, 0], fw_r.at[e, 0], (mate, col))
        c.start()
        return copies, [c]

    def gather_finish(e, buf, state):
        copies, forwards = state
        for i in range(1, ys):
            copies[i - 1].wait_recv()
            got = rows_of((y + ys - i) % ys, core)
            f = remote(buf.at[got, :], buf.at[got, :], fw_s.at[e, i], fw_r.at[e, i], (mate, col))
            f.start()
            forwards.append(f)
        for c in copies:
            c.wait_send()
        wait_all(forwards)

    def scatter_cols(e):
        copies = []
        for i in range(1, cols_n):
            other = (col + i) % cols_n
            rs = pl.ds(pl.multiple_of(other * block, block), block)
            so[e, i] = outp[rs, :].astype(BF16)
            c = remote(so.at[e, i], ro.at[e, i], ro_s.at[e, i], ro_r.at[e, i], (row, other))
            c.start()
            copies.append(c)
        return copies

    def scatter_finish(e, copies):
        acc = outp[my_rows, :]
        for i in range(1, cols_n):
            copies[i - 1].wait()
            acc = acc + ro[e, i].astype(F32)
        return acc

    def send_left(it, squares):
        p_buf[it, row, :, :width] = left[...]
        p_buf[it, row, :, width:] = jnp.broadcast_to(squares, (2, LANES))
        return row_send(p_buf.at[it], p_s.at[it], p_r.at[it])

    def send_right(it, squares):
        q_buf[it, col, :, :depth] = right[...]
        q_buf[it, col, :, depth:] = jnp.broadcast_to(squares, (2, LANES))
        return col_send(q_buf.at[it], q_s.at[it], q_r.at[it])

    def square_sum(vec):
        return jnp.sum(vec * vec, axis=1, keepdims=True)

    uvec[...] = u_start[...]
    loads[0].wait()
    times_left(0, uvec[0:1, :])
    loads[1].wait()
    times_left(1, uvec[1:2, :])
    p_copies = send_left(0, jnp.zeros((2, 1), F32))

    wait_all(tok_copies)
    matmul_nn(tok_all, w_in)
    first = reduce_first(0)

    wait_all(p_copies)
    left[...] = slot_sum(p_buf.at[0], rows_n)[:, :width]
    times_right(0, left[0:1, :])
    times_right(1, left[1:2, :])
    q_copies = send_right(0, square_sum(left[...]))

    second = reduce_second(0, first)

    wait_all(q_copies)
    summed = slot_sum(q_buf.at[0], cols_n)
    norm = jnp.sqrt(summed[:, depth : depth + 1] + EPSILON)
    uvec[...] = summed[:, :depth] / norm
    squares = square_sum(uvec[...])
    times_left(0, uvec[0:1, :])
    times_left(1, uvec[1:2, :])
    p_copies = send_left(1, squares)

    hid[...] = reduce_last(0, second)

    wait_all(p_copies)
    summed = slot_sum(p_buf.at[1], rows_n)
    sigma = jnp.sqrt(summed[:, width : width + 1] + EPSILON)
    left[...] = summed[:, :width] / sigma
    times_right(0, left[0:1, :])
    times_right(1, left[1:2, :])
    q_copies = send_right(1, square_sum(left[...]))
    wait_all(q_copies)
    summed = slot_sum(q_buf.at[1], cols_n)
    norm = jnp.sqrt(summed[:, depth : depth + 1] + EPSILON)
    v_units[...] = left[...] / norm
    uvec[...] = summed[:, :depth] / norm
    n_buf[row] = jnp.broadcast_to(square_sum(uvec[...]), (2, LANES))
    wait_all(row_send(n_buf, n_s, n_r))
    sigma = jnp.sqrt(slot_sum(n_buf, rows_n)[:, 0:1] + EPSILON)
    u_next[...] = uvec[...] / sigma
    scales = gains[:, 0:1] / sigma
    scale_in, scale_out = scales[0:1, :], scales[1:2, :]

    base = row * chunk

    def act_step(i, _):
        rs = pl.ds(pl.multiple_of(i * 16, 16), 16)
        h = hid[rs, :] * scale_in
        cdf = 0.5 * (1.0 + lax.erf(h * ROOT_HALF))
        slopes[rs, :] = cdf + h * jnp.exp(-0.5 * h * h) * INV_ROOT_TWO_PI
        act_all[pl.ds(pl.multiple_of(base + i * 16, 16), 16), :] = (h * cdf).astype(BF16)
        return 0

    lax.fori_loop(0, chunk // 16, act_step, 0)
    gather_finish(0, act_all, gather_rows(0, act_all))

    matmul_nt(act_all, w_out)
    output = scale_out * scatter_finish(0, scatter_cols(0))
    loss_scale = 1.0 / jnp.sqrt(jnp.float32(total))
    g_all[my_rows, :] = ((output - target[...].astype(F32)) * loss_scale).astype(BF16)
    g_copies = []
    for i in range(1, cols_n):
        c = remote(g_all.at[my_rows, :], g_all.at[my_rows, :], g_s.at[i], g_r.at[i],
                   (row, (col + i) % cols_n))
        c.start()
        g_copies.append(c)
    wait_all(g_copies)

    matmul_nn(g_all, w_out)
    own[...] = reduce_last(1, reduce_second(1, reduce_first(1)))

    def grad_step(i, sums):
        rs = pl.ds(pl.multiple_of(i * 16, 16), 16)
        ra = pl.ds(pl.multiple_of(base + i * 16, 16), 16)
        d = own[rs, :]
        grad = (scale_out * d * slopes[rs, :]).astype(BF16)
        gh_all[ra, :] = grad
        a = jnp.sum(grad.astype(F32) * hid[rs, :], axis=0, keepdims=True)
        b = jnp.sum(act_all[ra, :].astype(F32) * d, axis=0, keepdims=True)
        return sums[0] + a, sums[1] + b

    zero = jnp.zeros((1, width), F32)
    sum_in, sum_out = lax.fori_loop(0, chunk // 16, grad_step, (zero, zero))
    state = gather_rows(1, gh_all)
    tr_buf[row, 0:1] = jnp.broadcast_to(jnp.sum(sum_in, axis=1, keepdims=True), (1, LANES))
    tr_buf[row, 1:2] = jnp.broadcast_to(jnp.sum(sum_out, axis=1, keepdims=True), (1, LANES))
    wait_all(row_send(tr_buf, tr_s, tr_r))
    tc_buf[col] = slot_sum(tr_buf, rows_n)
    tc_copies = col_send(tc_buf, tc_s, tc_r)
    gather_finish(1, gh_all, state)

    matmul_nt(gh_all, w_in)
    copies = scatter_cols(1)
    wait_all(tc_copies)
    traces = slot_sum(tc_buf, cols_n)
    coeffs[0:2, :] = jnp.broadcast_to(scales, (2, LANES))
    coeffs[2:4, :] = scales * traces / sigma
    grad_tokens[...] = (scale_in * scatter_finish(1, copies)).astype(BF16)


def shards(rows_n, cols_n, tokens, target, w_in, w_out, gains, u_start):
    block, depth = tokens.shape
    width = w_in.shape[1]
    total = block * cols_n
    ys = rows_n // 2
    chunk = total // rows_n
    vmem = pl.BlockSpec(memory_space=pltpu.VMEM)
    dma = pltpu.SemaphoreType.DMA
    S = pltpu.VMEM
    wide_gains = jnp.broadcast_to(gains[:, None], (2, LANES))
    tok_all, act_all, g_all, gh_all, u_next, v_units, coeffs, grad_tokens = pl.pallas_call(
        functools.partial(body, rows_n, cols_n),
        out_shape=(
            jax.ShapeDtypeStruct((total, depth), BF16),
            jax.ShapeDtypeStruct((total, width), BF16),
            jax.ShapeDtypeStruct((total, depth), BF16),
            jax.ShapeDtypeStruct((total, width), BF16),
            jax.ShapeDtypeStruct((2, depth), F32),
            jax.ShapeDtypeStruct((2, width), F32),
            jax.ShapeDtypeStruct((4, LANES), F32),
            jax.ShapeDtypeStruct((block, depth), BF16),
        ),
        in_specs=[vmem] * 4 + [pl.BlockSpec(memory_space=pl.ANY)] * 2,
        out_specs=[vmem] * 8,
        scratch_shapes=[
            S((depth, width), BF16), S((depth, width), BF16),
            S((total, width), F32),
            S((chunk, width), F32), S((chunk, width), F32), S((chunk, width), F32),
            S((2, ys, chunk, width), BF16), S((2, ys, chunk, width), BF16),
            S((2, ys, chunk, width), BF16), S((2, ys, chunk, width), BF16),
            S((total, depth), F32),
            S((2, cols_n, block, depth), BF16), S((2, cols_n, block, depth), BF16),
            S((16, depth), BF16), S((16, width), BF16),
            S((2, depth), F32), S((2, width), F32), S((2, depth), F32),
            S((2, rows_n, 2, width + LANES), F32),
            S((2, cols_n, 2, depth + LANES), F32),
            S((rows_n, 2, LANES), F32), S((rows_n, 2, LANES), F32), S((cols_n, 2, LANES), F32),
            dma((2,)), dma((2,)),
            dma((cols_n,)), dma((cols_n,)),
            dma((2, rows_n)), dma((2, rows_n)),
            dma((2, cols_n)), dma((2, cols_n)),
            dma((rows_n,)), dma((rows_n,)),
            dma((rows_n,)), dma((rows_n,)),
            dma((cols_n,)), dma((cols_n,)),
            dma((2, ys)), dma((2, ys)),
            dma((2, ys)), dma((2, ys)),
            dma((2, ys)), dma((2, ys)),
            dma((2, ys)), dma((2, ys)),
            dma((2, cols_n)), dma((2, cols_n)),
            dma((cols_n,)), dma((cols_n,)),
        ],
        compiler_params=pltpu.CompilerParams(
            collective_id=0, has_side_effects=True, vmem_limit_bytes=58 * 1024 * 1024
        ),
    )(tokens, target, wide_gains, u_start, w_in, w_out)
    block_in = lax.dot_general(
        tok_all, gh_all, (((0,), (0,)), ((), ())), preferred_element_type=F32
    )
    block_out = lax.dot_general(
        g_all, act_all, (((0,), (0,)), ((), ())), preferred_element_type=F32
    )
    grad_in = coeffs[0, 0] * block_in - coeffs[2, 0] * (u_next[0][:, None] * v_units[0][None, :])
    grad_out = coeffs[1, 0] * block_out - coeffs[3, 0] * (
        u_next[1][:, None] * v_units[1][None, :]
    )
    return grad_tokens, grad_in.astype(BF16), grad_out.astype(BF16), u_next


def solution(mesh):
    placed = (
        P("col", "row"),
        P("col", "row"),
        P("row", "col"),
        P("row", "col"),
        P(),
        P(None, "row"),
    )
    return jax.shard_map(
        functools.partial(shards, mesh.shape["row"], mesh.shape["col"]),
        mesh=mesh,
        in_specs=placed,
        out_specs=(P("col", "row"), P("row", "col"), P("row", "col"), P(None, "row")),
        check_vma=False,
    )
```

```python
import functools

import jax
import jax.numpy as jnp
from jax import lax
from jax.experimental import pallas as pl
from jax.experimental.pallas import tpu as pltpu
from jax.sharding import PartitionSpec as P

POWER = 2
EPSILON = 1e-06
ROOT_HALF = 0.7071067811865476
INV_ROOT_TWO_PI = 0.3989422804014327
BF16 = jnp.bfloat16
F32 = jnp.float32
MESH = pl.DeviceIdType.MESH
LANES = 128


PARTS = 2


def tile_of(n):
    for t in (512, 256, 384):
        if n % t == 0:
            return t
    return LANES


def pieces(vec):
    high = vec.astype(BF16).astype(F32)
    rest = vec - high
    mid = rest.astype(BF16).astype(F32)
    low = rest - mid
    row = lax.broadcasted_iota(jnp.int32, (16, vec.shape[1]), 0)
    stacked = jnp.where(row == 0, high, jnp.where(row == 1, mid, jnp.where(row == 2, low, 0.0)))
    return stacked.astype(BF16)


def body(
    rows_n, cols_n,
    tokens, target, gains, u_start, w_in_hbm, w_out_hbm,
    tok_all, act_all, g_all, gh_all, u_next, v_units, coeffs, grad_tokens,
    w_in, w_out, part, slopes, hid, own, rs1, rr1, rs2, rr2, outp, out_own, cs1, cr1, cs2, cr2,
    pieces_l, pieces_r, left, right, p_buf, q_buf, n_buf, tr_buf, tc_buf,
    w_sem, p_s, p_r, q_s, q_r, n_s, n_r, tr_s, tr_r, tc_s, tc_r,
    rs1_s, rs1_r, rs2_s, rs2_r, cs1_s, cs1_r, cs2_s, cs2_r,
    rg_s, rg_r, rf_s, rf_r, cg_s, cg_r, cf_s, cf_r,
):
    row, col = lax.axis_index("row"), lax.axis_index("col")
    depth, width = w_in.shape
    total = tok_all.shape[0]
    block = total // cols_n
    chunk = total // rows_n

    loads = [
        pltpu.make_async_copy(w_in_hbm, w_in, w_sem.at[0]),
        pltpu.make_async_copy(w_out_hbm, w_out, w_sem.at[1]),
    ]
    for load in loads:
        load.start()

    def on_row(i):
        return (i, col)

    def on_col(i):
        return (row, i)

    barrier = pltpu.get_barrier_semaphore()
    for i in range(1, rows_n):
        pl.semaphore_signal(
            barrier, inc=1, device_id=on_row((row + i) % rows_n), device_id_type=MESH
        )
    for i in range(1, cols_n):
        pl.semaphore_signal(
            barrier, inc=1, device_id=on_col((col + i) % cols_n), device_id_type=MESH
        )
    pl.semaphore_wait(barrier, rows_n + cols_n - 2)

    def remote(src, dst, send, recv, dev):
        return pltpu.make_async_remote_copy(
            src_ref=src, dst_ref=dst, send_sem=send, recv_sem=recv, device_id=dev,
            device_id_type=MESH,
        )

    def all_send(n, me, dev, buf, send, recv):
        copies = []
        for i in range(1, n):
            c = remote(buf.at[me], buf.at[me], send.at[i], recv.at[i], dev((me + i) % n))
            c.start()
            copies.append(c)
        return copies

    row_send = functools.partial(all_send, rows_n, row, on_row)
    col_send = functools.partial(all_send, cols_n, col, on_col)

    def wait_all(copies):
        for c in copies:
            c.wait()

    def slot_sum(buf, n):
        acc = buf[0]
        for j in range(1, n):
            acc = acc + buf[j]
        return acc

    class Axis:
        def __init__(self, n, me, dev, size, bufs, sems, gather_sems):
            self.count, self.size, self.dev = n // 2, size, dev
            self.high, self.low = me // 2, me % 2
            self.mate = dev(self.high * 2 + 1 - self.low)
            self.bufs, self.sems, self.gather_sems = bufs, sems, gather_sems

        def rows(self, high, low):
            return pl.ds(pl.multiple_of((high * 2 + low) * self.size, self.size), self.size)

        def first(self, e, h, src):
            s1, r1 = self.bufs[:2]
            s_s, s_r = self.sems[:2]
            cols = half(src.shape[1], h)
            copies = []
            for i in range(1, self.count + 1):
                other = (self.high + i) % self.count
                s1[e, h, i - 1] = src[self.rows(other, 1 - self.low), cols].astype(BF16)
                c = remote(s1.at[e, h, i - 1], r1.at[e, h, i - 1], s_s.at[e, h, i - 1],
                           s_r.at[e, h, i - 1], self.mate)
                c.start()
                copies.append(c)
            return copies

        def second(self, e, h, src, dst, copies):
            s2, r2 = self.bufs[2:]
            r1 = self.bufs[1]
            s_s, s_r = self.sems[2:]
            cols = half(src.shape[1], h)
            sent = []
            for i in range(1, self.count):
                copies[i - 1].wait()
                other = (self.high + i) % self.count
                s2[e, h, i - 1] = (
                    src[self.rows(other, self.low), cols] + r1[e, h, i - 1].astype(F32)
                ).astype(BF16)
                c = remote(s2.at[e, h, i - 1], r2.at[e, h, i - 1], s_s.at[e, h, i - 1],
                           s_r.at[e, h, i - 1], self.dev(other * 2 + self.low))
                c.start()
                sent.append(c)
            copies[-1].wait()
            dst[:, cols] = (
                src[self.rows(self.high, self.low), cols]
                + r1[e, h, self.count - 1].astype(F32)
            )
            return sent

        def last(self, e, h, dst, sent):
            r2 = self.bufs[3]
            cols = half(dst.shape[1], h)
            wait_all(sent)
            acc = dst[:, cols]
            for i in range(1, self.count):
                acc = acc + r2[e, h, i - 1].astype(F32)
            dst[:, cols] = acc

        def gather(self, e, buf):
            g_s, g_r, f_s, f_r = self.gather_sems
            mine = buf.at[self.rows(self.high, self.low), :]
            copies = []
            for i in range(1, self.count):
                c = remote(mine, mine, g_s.at[e, i], g_r.at[e, i],
                           self.dev(((self.high + i) % self.count) * 2 + self.low))
                c.start()
                copies.append(c)
            c = remote(mine, mine, f_s.at[e, 0], f_r.at[e, 0], self.mate)
            c.start()
            return e, buf, copies, c

        def finish(self, state):
            e, buf, copies, c0 = state
            g_s, g_r, f_s, f_r = self.gather_sems
            forwards = [c0]
            for i in range(1, self.count):
                copies[i - 1].wait_recv()
                got = buf.at[self.rows((self.high + self.count - i) % self.count, self.low), :]
                f = remote(got, got, f_s.at[e, i], f_r.at[e, i], self.mate)
                f.start()
                forwards.append(f)
            for c in copies:
                c.wait_send()
            wait_all(forwards)

    def half(n, h):
        return pl.ds(h * (n // PARTS), n // PARTS)

    rowx = Axis(rows_n, row, on_row, chunk, (rs1, rr1, rs2, rr2),
                (rs1_s, rs1_r, rs2_s, rs2_r), (rg_s, rg_r, rf_s, rf_r))
    colx = Axis(cols_n, col, on_col, block, (cs1, cr1, cs2, cr2),
                (cs1_s, cs1_r, cs2_s, cs2_r), (cg_s, cg_r, cf_s, cf_r))

    my_rows = pl.ds(pl.multiple_of(col * block, block), block)
    tok_all[my_rows, :] = tokens[...]
    tok_state = colx.gather(0, tok_all)

    weights = (w_in, w_out)

    def times_left(k, vec):
        pieces_l[...] = pieces(vec)
        t = tile_of(width)

        def step(i, _):
            cs = pl.ds(pl.multiple_of(i * t, t), t)
            out = jnp.dot(pieces_l[...], weights[k][:, cs], preferred_element_type=F32)
            left[k, :, cs] = jnp.sum(out, axis=0, keepdims=True)
            return 0

        lax.fori_loop(0, width // t, step, 0)

    def times_right(k, vec):
        pieces_r[...] = pieces(vec)
        t = 256

        def step(i, _):
            rs = pl.ds(pl.multiple_of(i * t, t), t)
            out = lax.dot_general(
                pieces_r[...], weights[k][rs, :], (((1,), (1,)), ((), ())),
                preferred_element_type=F32,
            )
            right[k, :, rs] = jnp.sum(out, axis=0, keepdims=True)
            return 0

        lax.fori_loop(0, depth // t, step, 0)

    def matmul_nn(a, w, h):
        n = width // PARTS
        t = tile_of(n)

        def step(i, _):
            cs = pl.ds(pl.multiple_of(h * n + i * t, LANES), t)
            part[:, cs] = jnp.dot(a[...], w[:, cs], preferred_element_type=F32)
            return 0

        lax.fori_loop(0, n // t, step, 0)

    def matmul_nt(a, w, h):
        n = depth // PARTS
        t = tile_of(n)

        def step(i, _):
            cs = pl.ds(pl.multiple_of(h * n + i * t, LANES), t)
            outp[:, cs] = lax.dot_general(
                a[...], w[cs, :], (((1,), (1,)), ((), ())), preferred_element_type=F32
            )
            return 0

        lax.fori_loop(0, n // t, step, 0)

    def square_sum(vec):
        return jnp.sum(vec * vec, axis=1, keepdims=True)

    def send_left(it, k, squares):
        p_buf[it, k, row, :, :width] = left[k]
        p_buf[it, k, row, :, width:] = jnp.broadcast_to(squares, (1, LANES))
        return row_send(p_buf.at[it, k], p_s.at[it, k], p_r.at[it, k])

    def send_right(it, k, squares):
        q_buf[it, k, col, :, :depth] = right[k]
        q_buf[it, k, col, :, depth:] = jnp.broadcast_to(squares, (1, LANES))
        return col_send(q_buf.at[it, k], q_s.at[it, k], q_r.at[it, k])

    def right_half(it, k, copies):
        wait_all(copies)
        summed = slot_sum(p_buf.at[it, k], rows_n)
        vec = summed[:, :width]
        if it > 0:
            vec = vec / jnp.sqrt(summed[:, width : width + 1] + EPSILON)
        left[k] = vec
        times_right(k, vec)
        return send_right(it, k, square_sum(left[k]))

    def left_half(k, copies):
        wait_all(copies)
        summed = slot_sum(q_buf.at[0, k], cols_n)
        vec = summed[:, :depth] / jnp.sqrt(summed[:, depth : depth + 1] + EPSILON)
        times_left(k, vec)
        return send_left(1, k, square_sum(vec))

    def last_half(k, copies):
        wait_all(copies)
        summed = slot_sum(q_buf.at[1, k], cols_n)
        norm = jnp.sqrt(summed[:, depth : depth + 1] + EPSILON)
        v_units[k : k + 1, :] = left[k] / norm
        right[k] = summed[:, :depth] / norm
        n_buf[k, row] = jnp.broadcast_to(square_sum(right[k]), (1, LANES))
        return row_send(n_buf.at[k], n_s.at[k], n_r.at[k])

    def sigma_of(k, copies):
        wait_all(copies)
        sigma = jnp.sqrt(slot_sum(n_buf.at[k], rows_n)[:, 0:1] + EPSILON)
        u_next[k : k + 1, :] = right[k] / sigma
        return sigma, gains[k] / sigma

    zero = jnp.zeros((1, 1), F32)
    loads[0].wait()
    times_left(0, u_start[0:1, :])
    p0 = send_left(0, 0, zero)
    loads[1].wait()
    times_left(1, u_start[1:2, :])
    p1 = send_left(0, 1, zero)
    q0 = right_half(0, 0, p0)
    colx.finish(tok_state)
    matmul_nn(tok_all, w_in, 0)
    f0 = rowx.first(0, 0, part)
    q1 = right_half(0, 1, p1)
    p0 = left_half(0, q0)
    matmul_nn(tok_all, w_in, 1)
    f1 = rowx.first(0, 1, part)
    s0 = rowx.second(0, 0, part, hid, f0)
    p1 = left_half(1, q1)
    q0 = right_half(1, 0, p0)
    s1 = rowx.second(0, 1, part, hid, f1)
    q1 = right_half(1, 1, p1)
    n0 = last_half(0, q0)
    rowx.last(0, 0, hid, s0)
    rowx.last(0, 1, hid, s1)
    sigma_in, scale_in = sigma_of(0, n0)

    base = row * chunk

    def act_step(i, _):
        rs = pl.ds(pl.multiple_of(i * 16, 16), 16)
        h = hid[rs, :] * scale_in
        cdf = 0.5 * (1.0 + lax.erf(h * ROOT_HALF))
        slopes[rs, :] = cdf + h * jnp.exp(-0.5 * h * h) * INV_ROOT_TWO_PI
        act_all[pl.ds(pl.multiple_of(base + i * 16, 16), 16), :] = (h * cdf).astype(BF16)
        return 0

    lax.fori_loop(0, chunk // 16, act_step, 0)
    state = rowx.gather(0, act_all)
    n1 = last_half(1, q1)
    rowx.finish(state)

    matmul_nt(act_all, w_out, 0)
    f0 = colx.first(0, 0, outp)
    matmul_nt(act_all, w_out, 1)
    f1 = colx.first(0, 1, outp)
    sigma_out, scale_out = sigma_of(1, n1)
    s0 = colx.second(0, 0, outp, out_own, f0)
    s1 = colx.second(0, 1, outp, out_own, f1)
    colx.last(0, 0, out_own, s0)
    colx.last(0, 1, out_own, s1)
    loss_scale = 1.0 / jnp.sqrt(jnp.float32(total))
    g_all[my_rows, :] = (
        (scale_out * out_own[...] - target[...].astype(F32)) * loss_scale
    ).astype(BF16)
    colx.finish(colx.gather(1, g_all))

    matmul_nn(g_all, w_out, 0)
    f0 = rowx.first(1, 0, part)
    matmul_nn(g_all, w_out, 1)
    f1 = rowx.first(1, 1, part)
    s0 = rowx.second(1, 0, part, own, f0)
    s1 = rowx.second(1, 1, part, own, f1)
    rowx.last(1, 0, own, s0)
    rowx.last(1, 1, own, s1)

    def grad_step(i, sums):
        rs = pl.ds(pl.multiple_of(i * 16, 16), 16)
        ra = pl.ds(pl.multiple_of(base + i * 16, 16), 16)
        d = own[rs, :]
        grad = (scale_out * d * slopes[rs, :]).astype(BF16)
        gh_all[ra, :] = grad
        a = jnp.sum(grad.astype(F32) * hid[rs, :], axis=0, keepdims=True)
        b = jnp.sum(act_all[ra, :].astype(F32) * d, axis=0, keepdims=True)
        return sums[0] + a, sums[1] + b

    zeros = jnp.zeros((1, width), F32)
    sum_in, sum_out = lax.fori_loop(0, chunk // 16, grad_step, (zeros, zeros))
    state = rowx.gather(1, gh_all)
    tr_buf[row, 0:1] = jnp.broadcast_to(jnp.sum(sum_in, axis=1, keepdims=True), (1, LANES))
    tr_buf[row, 1:2] = jnp.broadcast_to(jnp.sum(sum_out, axis=1, keepdims=True), (1, LANES))
    tr_copies = row_send(tr_buf, tr_s, tr_r)
    rowx.finish(state)
    wait_all(tr_copies)
    tc_buf[col] = slot_sum(tr_buf, rows_n)
    tc_copies = col_send(tc_buf, tc_s, tc_r)

    matmul_nt(gh_all, w_in, 0)
    f0 = colx.first(1, 0, outp)
    matmul_nt(gh_all, w_in, 1)
    f1 = colx.first(1, 1, outp)
    s0 = colx.second(1, 0, outp, out_own, f0)
    s1 = colx.second(1, 1, outp, out_own, f1)
    wait_all(tc_copies)
    traces = slot_sum(tc_buf, cols_n)
    coeffs[0:1, :] = jnp.broadcast_to(scale_in, (1, LANES))
    coeffs[1:2, :] = jnp.broadcast_to(scale_out, (1, LANES))
    coeffs[2:3, :] = scale_in * traces[0:1] / sigma_in
    coeffs[3:4, :] = scale_out * traces[1:2] / sigma_out
    colx.last(1, 0, out_own, s0)
    colx.last(1, 1, out_own, s1)
    grad_tokens[...] = (scale_in * out_own[...]).astype(BF16)


def grads_body(tok, gh, g, act, u, v, coeffs, gin, gout):
    width = gh.shape[1]
    t = tile_of(width)
    for k, (a, b, out) in enumerate(((tok, gh, gin), (g, act, gout))):
        turned = jnp.transpose(a[...])
        shift = jnp.broadcast_to(u[k : k + 1, :] * coeffs[2 + k : 3 + k, 0:1], (LANES, u.shape[1]))
        shift = jnp.transpose(shift)[:, 0:1]
        scale = coeffs[k : k + 1, 0:1]
        for i in range(width // t):
            cs = slice(i * t, (i + 1) * t)
            prod = jnp.dot(turned, b[:, cs], preferred_element_type=F32)
            out[:, cs] = (scale * prod - shift * v[k : k + 1, cs]).astype(BF16)


def shards(rows_n, cols_n, tokens, target, w_in, w_out, gains, u_start):
    block, depth = tokens.shape
    width = w_in.shape[1]
    total = block * cols_n
    chunk = total // rows_n
    vmem = pl.BlockSpec(memory_space=pltpu.VMEM)
    dma = pltpu.SemaphoreType.DMA
    S = pltpu.VMEM
    ys, zs = rows_n // 2, cols_n // 2
    row_part = (2, PARTS, ys, chunk, width // PARTS)
    col_part = (2, PARTS, zs, block, depth // PARTS)
    tok_all, act_all, g_all, gh_all, u_next, v_units, coeffs, grad_tokens = pl.pallas_call(
        functools.partial(body, rows_n, cols_n),
        out_shape=(
            jax.ShapeDtypeStruct((total, depth), BF16),
            jax.ShapeDtypeStruct((total, width), BF16),
            jax.ShapeDtypeStruct((total, depth), BF16),
            jax.ShapeDtypeStruct((total, width), BF16),
            jax.ShapeDtypeStruct((2, depth), F32),
            jax.ShapeDtypeStruct((2, width), F32),
            jax.ShapeDtypeStruct((4, LANES), F32),
            jax.ShapeDtypeStruct((block, depth), BF16),
        ),
        in_specs=[vmem, vmem, pl.BlockSpec(memory_space=pltpu.SMEM), vmem]
        + [pl.BlockSpec(memory_space=pl.ANY)] * 2,
        out_specs=[vmem] * 8,
        scratch_shapes=[
            S((depth, width), BF16), S((depth, width), BF16),
            S((total, width), F32),
            S((chunk, width), F32), S((chunk, width), F32), S((chunk, width), F32),
            S(row_part, BF16), S(row_part, BF16), S(row_part, BF16), S(row_part, BF16),
            S((total, depth), F32), S((block, depth), F32),
            S(col_part, BF16), S(col_part, BF16), S(col_part, BF16), S(col_part, BF16),
            S((16, depth), BF16), S((16, width), BF16),
            S((2, 1, width), F32), S((2, 1, depth), F32),
            S((2, 2, rows_n, 1, width + LANES), F32),
            S((2, 2, cols_n, 1, depth + LANES), F32),
            S((2, rows_n, 1, LANES), F32), S((rows_n, 2, LANES), F32), S((cols_n, 2, LANES), F32),
            dma((2,)),
            dma((2, 2, rows_n)), dma((2, 2, rows_n)),
            dma((2, 2, cols_n)), dma((2, 2, cols_n)),
            dma((2, rows_n)), dma((2, rows_n)),
            dma((rows_n,)), dma((rows_n,)),
            dma((cols_n,)), dma((cols_n,)),
        ]
        + [dma((2, PARTS, ys))] * 4
        + [dma((2, PARTS, zs))] * 4
        + [dma((2, ys))] * 4
        + [dma((2, zs))] * 4,
        compiler_params=pltpu.CompilerParams(
            collective_id=0, has_side_effects=True, vmem_limit_bytes=58 * 1024 * 1024
        ),
    )(tokens, target, gains, u_start, w_in, w_out)
    rows = 256
    whole = lambda shape: pl.BlockSpec(shape, lambda i: (0, 0))
    side = lambda n: pl.BlockSpec((n, rows), lambda i: (0, i))
    grad_in, grad_out = pl.pallas_call(
        grads_body,
        grid=(depth // rows,),
        out_shape=(
            jax.ShapeDtypeStruct((depth, width), BF16),
            jax.ShapeDtypeStruct((depth, width), BF16),
        ),
        in_specs=[
            side(total), whole((total, width)), side(total), whole((total, width)),
            side(2), whole((2, width)), whole((4, LANES)),
        ],
        out_specs=[pl.BlockSpec((rows, width), lambda i: (i, 0))] * 2,
        compiler_params=pltpu.CompilerParams(vmem_limit_bytes=40 * 1024 * 1024),
    )(tok_all, gh_all, g_all, act_all, u_next, v_units, coeffs)
    return grad_tokens, grad_in, grad_out, u_next


def solution(mesh):
    placed = (
        P("col", "row"),
        P("col", "row"),
        P("row", "col"),
        P("row", "col"),
        P(),
        P(None, "row"),
    )
    return jax.shard_map(
        functools.partial(shards, mesh.shape["row"], mesh.shape["col"]),
        mesh=mesh,
        in_specs=placed,
        out_specs=(P("col", "row"), P("row", "col"), P("row", "col"), P(None, "row")),
        check_vma=False,
    )
```

```python
import functools

import jax
import jax.numpy as jnp
from jax import lax
from jax.experimental import pallas as pl
from jax.experimental.pallas import tpu as pltpu
from jax.sharding import PartitionSpec as P

POWER = 2
EPSILON = 1e-06
ROOT_HALF = 0.7071067811865476
INV_ROOT_TWO_PI = 0.3989422804014327
BF16 = jnp.bfloat16
F32 = jnp.float32
MESH = pl.DeviceIdType.MESH
LANES = 128


PARTS = 2


def tile_of(n):
    for t in (512, 256, 384):
        if n % t == 0:
            return t
    return LANES


def pieces(vec):
    high = vec.astype(BF16).astype(F32)
    rest = vec - high
    mid = rest.astype(BF16).astype(F32)
    low = rest - mid
    row = lax.broadcasted_iota(jnp.int32, (16, vec.shape[1]), 0)
    stacked = jnp.where(row == 0, high, jnp.where(row == 1, mid, jnp.where(row == 2, low, 0.0)))
    return stacked.astype(BF16)


def body(
    rows_n, cols_n,
    tokens, target, gains, u_start, w_in_hbm, w_out_hbm,
    tok_all, act_all, g_all, gh_all, u_next, v_units, coeffs, grad_tokens,
    w_in, w_out, part, slopes, hid, own, rs1, rr1, rs2, rr2, outp, out_own, cs1, cr1, cs2, cr2,
    pieces_l, pieces_r, left, right, p_buf, q_buf, n_buf, tr_buf, tc_buf,
    w_sem, p_s, p_r, q_s, q_r, n_s, n_r, tr_s, tr_r, tc_s, tc_r,
    rs1_s, rs1_r, rs2_s, rs2_r, cs1_s, cs1_r, cs2_s, cs2_r,
    rg_s, rg_r, rf_s, rf_r, cg_s, cg_r, cf_s, cf_r,
):
    row, col = lax.axis_index("row"), lax.axis_index("col")
    depth, width = w_in.shape
    total = tok_all.shape[0]
    block = total // cols_n
    chunk = total // rows_n

    loads = [
        pltpu.make_async_copy(w_in_hbm, w_in, w_sem.at[0]),
        pltpu.make_async_copy(w_out_hbm, w_out, w_sem.at[1]),
    ]
    for load in loads:
        load.start()

    def on_row(i):
        return (i, col)

    def on_col(i):
        return (row, i)

    barrier = pltpu.get_barrier_semaphore()
    for i in range(1, rows_n):
        pl.semaphore_signal(
            barrier, inc=1, device_id=on_row((row + i) % rows_n), device_id_type=MESH
        )
    for i in range(1, cols_n):
        pl.semaphore_signal(
            barrier, inc=1, device_id=on_col((col + i) % cols_n), device_id_type=MESH
        )
    pl.semaphore_wait(barrier, rows_n + cols_n - 2)

    def remote(src, dst, send, recv, dev):
        return pltpu.make_async_remote_copy(
            src_ref=src, dst_ref=dst, send_sem=send, recv_sem=recv, device_id=dev,
            device_id_type=MESH,
        )

    def all_send(n, me, dev, buf, send, recv):
        copies = []
        for i in range(1, n):
            c = remote(buf.at[me], buf.at[me], send.at[i], recv.at[i], dev((me + i) % n))
            c.start()
            copies.append(c)
        return copies

    row_send = functools.partial(all_send, rows_n, row, on_row)
    col_send = functools.partial(all_send, cols_n, col, on_col)

    def wait_all(copies):
        for c in copies:
            c.wait()

    def slot_sum(buf, n):
        acc = buf[0]
        for j in range(1, n):
            acc = acc + buf[j]
        return acc

    class Axis:
        def __init__(self, n, me, dev, size, bufs, sems, gather_sems):
            self.count, self.size, self.dev = n // 2, size, dev
            self.high, self.low = me // 2, me % 2
            self.mate = dev(self.high * 2 + 1 - self.low)
            self.bufs, self.sems, self.gather_sems = bufs, sems, gather_sems

        def rows(self, high, low):
            return pl.ds(pl.multiple_of((high * 2 + low) * self.size, self.size), self.size)

        def first(self, e, h, src):
            s1, r1 = self.bufs[:2]
            s_s, s_r = self.sems[:2]
            cols = half(src.shape[1], h)
            copies = []
            for i in range(1, self.count + 1):
                other = (self.high + i) % self.count
                s1[e, h, i - 1] = src[self.rows(other, 1 - self.low), cols].astype(BF16)
                c = remote(s1.at[e, h, i - 1], r1.at[e, h, i - 1], s_s.at[e, h, i - 1],
                           s_r.at[e, h, i - 1], self.mate)
                c.start()
                copies.append(c)
            return copies

        def second(self, e, h, src, dst, copies):
            s2, r2 = self.bufs[2:]
            r1 = self.bufs[1]
            s_s, s_r = self.sems[2:]
            cols = half(src.shape[1], h)
            sent = []
            for i in range(1, self.count):
                copies[i - 1].wait()
                other = (self.high + i) % self.count
                s2[e, h, i - 1] = (
                    src[self.rows(other, self.low), cols] + r1[e, h, i - 1].astype(F32)
                ).astype(BF16)
                c = remote(s2.at[e, h, i - 1], r2.at[e, h, i - 1], s_s.at[e, h, i - 1],
                           s_r.at[e, h, i - 1], self.dev(other * 2 + self.low))
                c.start()
                sent.append(c)
            copies[-1].wait()
            dst[:, cols] = (
                src[self.rows(self.high, self.low), cols]
                + r1[e, h, self.count - 1].astype(F32)
            )
            return sent

        def last(self, e, h, dst, sent):
            r2 = self.bufs[3]
            cols = half(dst.shape[1], h)
            wait_all(sent)
            acc = dst[:, cols]
            for i in range(1, self.count):
                acc = acc + r2[e, h, i - 1].astype(F32)
            dst[:, cols] = acc

        def piece(self, high, h):
            n = self.size // PARTS
            start = (high * 2 + self.low) * self.size + h * n
            return pl.ds(pl.multiple_of(start, n), n)

        def gather(self, e, h, buf):
            g_s, g_r, f_s, f_r = self.gather_sems
            mine = buf.at[self.piece(self.high, h), :]
            copies = []
            for i in range(1, self.count):
                c = remote(mine, mine, g_s.at[e, h, i], g_r.at[e, h, i],
                           self.dev(((self.high + i) % self.count) * 2 + self.low))
                c.start()
                copies.append(c)
            c = remote(mine, mine, f_s.at[e, h, 0], f_r.at[e, h, 0], self.mate)
            c.start()
            return e, h, buf, copies, c

        def forward(self, states):
            g_s, g_r, f_s, f_r = self.gather_sems
            forwards = []
            for e, h, buf, copies, c0 in states:
                forwards.append(c0)
                for i in range(1, self.count):
                    copies[i - 1].wait_recv()
                    got = buf.at[self.piece((self.high + self.count - i) % self.count, h), :]
                    f = remote(got, got, f_s.at[e, h, i], f_r.at[e, h, i], self.mate)
                    f.start()
                    forwards.append(f)
            return states, forwards

        def complete(self, moves):
            states, forwards = moves
            for _, _, _, copies, _ in states:
                for c in copies:
                    c.wait_send()
            wait_all(forwards)

        def finish(self, states):
            self.complete(self.forward(states))

        def gather_all(self, e, buf):
            return [self.gather(e, h, buf) for h in range(PARTS)]

    def half(n, h):
        return pl.ds(h * (n // PARTS), n // PARTS)

    rowx = Axis(rows_n, row, on_row, chunk, (rs1, rr1, rs2, rr2),
                (rs1_s, rs1_r, rs2_s, rs2_r), (rg_s, rg_r, rf_s, rf_r))
    colx = Axis(cols_n, col, on_col, block, (cs1, cr1, cs2, cr2),
                (cs1_s, cs1_r, cs2_s, cs2_r), (cg_s, cg_r, cf_s, cf_r))

    my_rows = pl.ds(pl.multiple_of(col * block, block), block)
    tok_all[my_rows, :] = tokens[...]
    tok_state = colx.gather_all(0, tok_all)

    weights = (w_in, w_out)

    def times_left(k, vec):
        pieces_l[...] = pieces(vec)
        t = tile_of(width)

        def step(i, _):
            cs = pl.ds(pl.multiple_of(i * t, t), t)
            out = jnp.dot(pieces_l[...], weights[k][:, cs], preferred_element_type=F32)
            left[k, :, cs] = jnp.sum(out, axis=0, keepdims=True)
            return 0

        lax.fori_loop(0, width // t, step, 0)

    def times_right(k, vec):
        pieces_r[...] = pieces(vec)
        t = 256

        def step(i, _):
            rs = pl.ds(pl.multiple_of(i * t, t), t)
            out = lax.dot_general(
                pieces_r[...], weights[k][rs, :], (((1,), (1,)), ((), ())),
                preferred_element_type=F32,
            )
            right[k, :, rs] = jnp.sum(out, axis=0, keepdims=True)
            return 0

        lax.fori_loop(0, depth // t, step, 0)

    def matmul_nn(a, w, h):
        n = width // PARTS
        t = tile_of(n)

        def step(i, _):
            cs = pl.ds(pl.multiple_of(h * n + i * t, LANES), t)
            part[:, cs] = jnp.dot(a[...], w[:, cs], preferred_element_type=F32)
            return 0

        lax.fori_loop(0, n // t, step, 0)

    def matmul_nt(a, w, h):
        n = depth // PARTS
        t = tile_of(n)

        def step(i, _):
            cs = pl.ds(pl.multiple_of(h * n + i * t, LANES), t)
            outp[:, cs] = lax.dot_general(
                a[...], w[cs, :], (((1,), (1,)), ((), ())), preferred_element_type=F32
            )
            return 0

        lax.fori_loop(0, n // t, step, 0)

    def square_sum(vec):
        return jnp.sum(vec * vec, axis=1, keepdims=True)

    def send_left(it, k, squares):
        p_buf[it, k, row, :, :width] = left[k]
        p_buf[it, k, row, :, width:] = jnp.broadcast_to(squares, (1, LANES))
        return row_send(p_buf.at[it, k], p_s.at[it, k], p_r.at[it, k])

    def send_right(it, k, squares):
        q_buf[it, k, col, :, :depth] = right[k]
        q_buf[it, k, col, :, depth:] = jnp.broadcast_to(squares, (1, LANES))
        return col_send(q_buf.at[it, k], q_s.at[it, k], q_r.at[it, k])

    def right_half(it, k, copies):
        wait_all(copies)
        summed = slot_sum(p_buf.at[it, k], rows_n)
        vec = summed[:, :width]
        if it > 0:
            vec = vec / jnp.sqrt(summed[:, width : width + 1] + EPSILON)
        left[k] = vec
        times_right(k, vec)
        return send_right(it, k, square_sum(left[k]))

    def left_half(k, copies):
        wait_all(copies)
        summed = slot_sum(q_buf.at[0, k], cols_n)
        vec = summed[:, :depth] / jnp.sqrt(summed[:, depth : depth + 1] + EPSILON)
        times_left(k, vec)
        return send_left(1, k, square_sum(vec))

    def last_half(k, copies):
        wait_all(copies)
        summed = slot_sum(q_buf.at[1, k], cols_n)
        norm = jnp.sqrt(summed[:, depth : depth + 1] + EPSILON)
        v_units[k : k + 1, :] = left[k] / norm
        right[k] = summed[:, :depth] / norm
        n_buf[k, row] = jnp.broadcast_to(square_sum(right[k]), (1, LANES))
        return row_send(n_buf.at[k], n_s.at[k], n_r.at[k])

    def sigma_of(k, copies):
        wait_all(copies)
        sigma = jnp.sqrt(slot_sum(n_buf.at[k], rows_n)[:, 0:1] + EPSILON)
        u_next[k : k + 1, :] = right[k] / sigma
        return sigma, gains[k] / sigma

    zero = jnp.zeros((1, 1), F32)
    loads[0].wait()
    times_left(0, u_start[0:1, :])
    p0 = send_left(0, 0, zero)
    loads[1].wait()
    times_left(1, u_start[1:2, :])
    p1 = send_left(0, 1, zero)
    tok_moves = colx.forward(tok_state)
    q0 = right_half(0, 0, p0)
    colx.complete(tok_moves)
    matmul_nn(tok_all, w_in, 0)
    f0 = rowx.first(0, 0, part)
    q1 = right_half(0, 1, p1)
    p0 = left_half(0, q0)
    matmul_nn(tok_all, w_in, 1)
    f1 = rowx.first(0, 1, part)
    s0 = rowx.second(0, 0, part, hid, f0)
    p1 = left_half(1, q1)
    q0 = right_half(1, 0, p0)
    s1 = rowx.second(0, 1, part, hid, f1)
    q1 = right_half(1, 1, p1)
    n0 = last_half(0, q0)
    rowx.last(0, 0, hid, s0)
    rowx.last(0, 1, hid, s1)
    sigma_in, scale_in = sigma_of(0, n0)

    base = row * chunk

    def act_step(i, _):
        rs = pl.ds(pl.multiple_of(i * 16, 16), 16)
        h = hid[rs, :] * scale_in
        cdf = 0.5 * (1.0 + lax.erf(h * ROOT_HALF))
        slopes[rs, :] = cdf + h * jnp.exp(-0.5 * h * h) * INV_ROOT_TWO_PI
        act_all[pl.ds(pl.multiple_of(base + i * 16, 16), 16), :] = (h * cdf).astype(BF16)
        return 0

    steps = chunk // 16 // PARTS
    state = []
    for h in range(PARTS):
        lax.fori_loop(h * steps, (h + 1) * steps, act_step, 0)
        state.append(rowx.gather(0, h, act_all))
    n1 = last_half(1, q1)
    rowx.finish(state)

    matmul_nt(act_all, w_out, 0)
    f0 = colx.first(0, 0, outp)
    matmul_nt(act_all, w_out, 1)
    f1 = colx.first(0, 1, outp)
    sigma_out, scale_out = sigma_of(1, n1)
    s0 = colx.second(0, 0, outp, out_own, f0)
    s1 = colx.second(0, 1, outp, out_own, f1)
    colx.last(0, 0, out_own, s0)
    colx.last(0, 1, out_own, s1)
    loss_scale = 1.0 / jnp.sqrt(jnp.float32(total))
    g_all[my_rows, :] = (
        (scale_out * out_own[...] - target[...].astype(F32)) * loss_scale
    ).astype(BF16)
    colx.finish(colx.gather_all(1, g_all))

    matmul_nn(g_all, w_out, 0)
    f0 = rowx.first(1, 0, part)
    matmul_nn(g_all, w_out, 1)
    f1 = rowx.first(1, 1, part)
    s0 = rowx.second(1, 0, part, own, f0)
    s1 = rowx.second(1, 1, part, own, f1)
    rowx.last(1, 0, own, s0)
    rowx.last(1, 1, own, s1)

    def grad_step(i, sums):
        rs = pl.ds(pl.multiple_of(i * 16, 16), 16)
        ra = pl.ds(pl.multiple_of(base + i * 16, 16), 16)
        d = own[rs, :]
        grad = (scale_out * d * slopes[rs, :]).astype(BF16)
        gh_all[ra, :] = grad
        a = jnp.sum(grad.astype(F32) * hid[rs, :], axis=0, keepdims=True)
        b = jnp.sum(act_all[ra, :].astype(F32) * d, axis=0, keepdims=True)
        return sums[0] + a, sums[1] + b

    zeros = jnp.zeros((1, width), F32)
    sums = (zeros, zeros)
    state = []
    for h in range(PARTS):
        sums = lax.fori_loop(h * steps, (h + 1) * steps, grad_step, sums)
        state.append(rowx.gather(1, h, gh_all))
    sum_in, sum_out = sums
    tr_buf[row, 0:1] = jnp.broadcast_to(jnp.sum(sum_in, axis=1, keepdims=True), (1, LANES))
    tr_buf[row, 1:2] = jnp.broadcast_to(jnp.sum(sum_out, axis=1, keepdims=True), (1, LANES))
    tr_copies = row_send(tr_buf, tr_s, tr_r)
    rowx.finish(state)
    wait_all(tr_copies)
    tc_buf[col] = slot_sum(tr_buf, rows_n)
    tc_copies = col_send(tc_buf, tc_s, tc_r)

    matmul_nt(gh_all, w_in, 0)
    f0 = colx.first(1, 0, outp)
    matmul_nt(gh_all, w_in, 1)
    f1 = colx.first(1, 1, outp)
    s0 = colx.second(1, 0, outp, out_own, f0)
    s1 = colx.second(1, 1, outp, out_own, f1)
    wait_all(tc_copies)
    traces = slot_sum(tc_buf, cols_n)
    coeffs[0:1, :] = jnp.broadcast_to(scale_in, (1, LANES))
    coeffs[1:2, :] = jnp.broadcast_to(scale_out, (1, LANES))
    coeffs[2:3, :] = scale_in * traces[0:1] / sigma_in
    coeffs[3:4, :] = scale_out * traces[1:2] / sigma_out
    colx.last(1, 0, out_own, s0)
    colx.last(1, 1, out_own, s1)
    grad_tokens[...] = (scale_in * out_own[...]).astype(BF16)


def grads_body(tok, gh, g, act, u, v, coeffs, gin, gout):
    width = gh.shape[1]
    t = tile_of(width)
    for k, (a, b, out) in enumerate(((tok, gh, gin), (g, act, gout))):
        turned = jnp.transpose(a[...])
        shift = jnp.broadcast_to(u[k : k + 1, :] * coeffs[2 + k : 3 + k, 0:1], (LANES, u.shape[1]))
        shift = jnp.transpose(shift)[:, 0:1]
        scale = coeffs[k : k + 1, 0:1]
        for i in range(width // t):
            cs = slice(i * t, (i + 1) * t)
            prod = jnp.dot(turned, b[:, cs], preferred_element_type=F32)
            out[:, cs] = (scale * prod - shift * v[k : k + 1, cs]).astype(BF16)


def shards(rows_n, cols_n, tokens, target, w_in, w_out, gains, u_start):
    block, depth = tokens.shape
    width = w_in.shape[1]
    total = block * cols_n
    chunk = total // rows_n
    vmem = pl.BlockSpec(memory_space=pltpu.VMEM)
    dma = pltpu.SemaphoreType.DMA
    S = pltpu.VMEM
    ys, zs = rows_n // 2, cols_n // 2
    row_part = (2, PARTS, ys, chunk, width // PARTS)
    col_part = (2, PARTS, zs, block, depth // PARTS)
    tok_all, act_all, g_all, gh_all, u_next, v_units, coeffs, grad_tokens = pl.pallas_call(
        functools.partial(body, rows_n, cols_n),
        out_shape=(
            jax.ShapeDtypeStruct((total, depth), BF16),
            jax.ShapeDtypeStruct((total, width), BF16),
            jax.ShapeDtypeStruct((total, depth), BF16),
            jax.ShapeDtypeStruct((total, width), BF16),
            jax.ShapeDtypeStruct((2, depth), F32),
            jax.ShapeDtypeStruct((2, width), F32),
            jax.ShapeDtypeStruct((4, LANES), F32),
            jax.ShapeDtypeStruct((block, depth), BF16),
        ),
        in_specs=[vmem, vmem, pl.BlockSpec(memory_space=pltpu.SMEM), vmem]
        + [pl.BlockSpec(memory_space=pl.ANY)] * 2,
        out_specs=[vmem] * 8,
        scratch_shapes=[
            S((depth, width), BF16), S((depth, width), BF16),
            S((total, width), F32),
            S((chunk, width), F32), S((chunk, width), F32), S((chunk, width), F32),
            S(row_part, BF16), S(row_part, BF16), S(row_part, BF16), S(row_part, BF16),
            S((total, depth), F32), S((block, depth), F32),
            S(col_part, BF16), S(col_part, BF16), S(col_part, BF16), S(col_part, BF16),
            S((16, depth), BF16), S((16, width), BF16),
            S((2, 1, width), F32), S((2, 1, depth), F32),
            S((2, 2, rows_n, 1, width + LANES), F32),
            S((2, 2, cols_n, 1, depth + LANES), F32),
            S((2, rows_n, 1, LANES), F32), S((rows_n, 2, LANES), F32), S((cols_n, 2, LANES), F32),
            dma((2,)),
            dma((2, 2, rows_n)), dma((2, 2, rows_n)),
            dma((2, 2, cols_n)), dma((2, 2, cols_n)),
            dma((2, rows_n)), dma((2, rows_n)),
            dma((rows_n,)), dma((rows_n,)),
            dma((cols_n,)), dma((cols_n,)),
        ]
        + [dma((2, PARTS, ys))] * 4
        + [dma((2, PARTS, zs))] * 4
        + [dma((2, PARTS, ys))] * 4
        + [dma((2, PARTS, zs))] * 4,
        compiler_params=pltpu.CompilerParams(
            collective_id=0, has_side_effects=True, vmem_limit_bytes=58 * 1024 * 1024
        ),
    )(tokens, target, gains, u_start, w_in, w_out)
    rows = 256
    whole = lambda shape: pl.BlockSpec(shape, lambda i: (0, 0))
    side = lambda n: pl.BlockSpec((n, rows), lambda i: (0, i))
    grad_in, grad_out = pl.pallas_call(
        grads_body,
        grid=(depth // rows,),
        out_shape=(
            jax.ShapeDtypeStruct((depth, width), BF16),
            jax.ShapeDtypeStruct((depth, width), BF16),
        ),
        in_specs=[
            side(total), whole((total, width)), side(total), whole((total, width)),
            side(2), whole((2, width)), whole((4, LANES)),
        ],
        out_specs=[pl.BlockSpec((rows, width), lambda i: (i, 0))] * 2,
        compiler_params=pltpu.CompilerParams(vmem_limit_bytes=60 * 1024 * 1024),
    )(tok_all, gh_all, g_all, act_all, u_next, v_units, coeffs)
    return grad_tokens, grad_in, grad_out, u_next


def solution(mesh):
    placed = (
        P("col", "row"),
        P("col", "row"),
        P("row", "col"),
        P("row", "col"),
        P(),
        P(None, "row"),
    )
    return jax.shard_map(
        functools.partial(shards, mesh.shape["row"], mesh.shape["col"]),
        mesh=mesh,
        in_specs=placed,
        out_specs=(P("col", "row"), P("row", "col"), P("row", "col"), P(None, "row")),
        check_vma=False,
    )
```

```python
import functools

import jax
import jax.numpy as jnp
from jax import lax
from jax.experimental import pallas as pl
from jax.experimental.pallas import tpu as pltpu
from jax.sharding import PartitionSpec as P

POWER = 2
EPSILON = 1e-06
ROOT_HALF = 0.7071067811865476
INV_ROOT_TWO_PI = 0.3989422804014327
BF16 = jnp.bfloat16
F32 = jnp.float32
MESH = pl.DeviceIdType.MESH
LANES = 128


PARTS = 2


def tile_of(n):
    for t in (512, 256, 384):
        if n % t == 0:
            return t
    return LANES


def pieces(vec):
    high = vec.astype(BF16).astype(F32)
    rest = vec - high
    mid = rest.astype(BF16).astype(F32)
    low = rest - mid
    row = lax.broadcasted_iota(jnp.int32, (16, vec.shape[1]), 0)
    stacked = jnp.where(row == 0, high, jnp.where(row == 1, mid, jnp.where(row == 2, low, 0.0)))
    return stacked.astype(BF16)


def body(
    rows_n, cols_n,
    tokens, target, gains, u_start, w_in_hbm, w_out_hbm,
    tok_all, act_all, g_all, gh_all, u_next, v_units, coeffs, grad_tokens,
    w_in, w_out, part, slopes, hid, own, rs1, rr1, rs2, rr2, outp, out_own, cs1, cr1, cs2, cr2,
    pieces_l, pieces_r, left, right, p_buf, q_buf, n_buf, tr_buf, tc_buf,
    w_sem, p_s, p_r, q_s, q_r, n_s, n_r, tr_s, tr_r, tc_s, tc_r,
    rs1_s, rs1_r, rs2_s, rs2_r, cs1_s, cs1_r, cs2_s, cs2_r,
    rg_s, rg_r, rf_s, rf_r, cg_s, cg_r, cf_s, cf_r,
):
    row, col = lax.axis_index("row"), lax.axis_index("col")
    depth, width = w_in.shape
    total = tok_all.shape[0]
    block = total // cols_n
    chunk = total // rows_n

    loads = [
        pltpu.make_async_copy(w_in_hbm, w_in, w_sem.at[0]),
        pltpu.make_async_copy(w_out_hbm, w_out, w_sem.at[1]),
    ]
    for load in loads:
        load.start()

    def on_row(i):
        return (i, col)

    def on_col(i):
        return (row, i)

    barrier = pltpu.get_barrier_semaphore()
    for i in range(1, rows_n):
        pl.semaphore_signal(
            barrier, inc=1, device_id=on_row((row + i) % rows_n), device_id_type=MESH
        )
    for i in range(1, cols_n):
        pl.semaphore_signal(
            barrier, inc=1, device_id=on_col((col + i) % cols_n), device_id_type=MESH
        )
    pl.semaphore_wait(barrier, rows_n + cols_n - 2)

    def remote(src, dst, send, recv, dev):
        return pltpu.make_async_remote_copy(
            src_ref=src, dst_ref=dst, send_sem=send, recv_sem=recv, device_id=dev,
            device_id_type=MESH,
        )

    def all_send(n, me, dev, buf, send, recv):
        copies = []
        for i in range(1, n):
            c = remote(buf.at[me], buf.at[me], send.at[i], recv.at[i], dev((me + i) % n))
            c.start()
            copies.append(c)
        return copies

    row_send = functools.partial(all_send, rows_n, row, on_row)
    col_send = functools.partial(all_send, cols_n, col, on_col)

    def wait_all(copies):
        for c in copies:
            c.wait()

    def slot_sum(buf, n):
        acc = buf[0]
        for j in range(1, n):
            acc = acc + buf[j]
        return acc

    class Axis:
        def __init__(self, n, me, dev, size, bufs, sems, gather_sems):
            self.count, self.size, self.dev = n // 2, size, dev
            self.high, self.low = me // 2, me % 2
            self.mate = dev(self.high * 2 + 1 - self.low)
            self.bufs, self.sems, self.gather_sems = bufs, sems, gather_sems

        def rows(self, high, low):
            return pl.ds(pl.multiple_of((high * 2 + low) * self.size, self.size), self.size)

        def first(self, e, h, src):
            s1, r1 = self.bufs[:2]
            s_s, s_r = self.sems[:2]
            cols = half(src.shape[1], h)
            copies = []
            for i in range(1, self.count + 1):
                other = (self.high + i) % self.count
                s1[e, h, i - 1] = src[self.rows(other, 1 - self.low), cols].astype(BF16)
                c = remote(s1.at[e, h, i - 1], r1.at[e, h, i - 1], s_s.at[e, h, i - 1],
                           s_r.at[e, h, i - 1], self.mate)
                c.start()
                copies.append(c)
            return copies

        def second(self, e, h, src, dst, copies):
            s2, r2 = self.bufs[2:]
            r1 = self.bufs[1]
            s_s, s_r = self.sems[2:]
            cols = half(src.shape[1], h)
            sent = []
            for i in range(1, self.count):
                copies[i - 1].wait()
                other = (self.high + i) % self.count
                s2[e, h, i - 1] = (
                    src[self.rows(other, self.low), cols] + r1[e, h, i - 1].astype(F32)
                ).astype(BF16)
                c = remote(s2.at[e, h, i - 1], r2.at[e, h, i - 1], s_s.at[e, h, i - 1],
                           s_r.at[e, h, i - 1], self.dev(other * 2 + self.low))
                c.start()
                sent.append(c)
            copies[-1].wait()
            dst[:, cols] = (
                src[self.rows(self.high, self.low), cols]
                + r1[e, h, self.count - 1].astype(F32)
            )
            return sent

        def last(self, e, h, dst, sent):
            r2 = self.bufs[3]
            cols = half(dst.shape[1], h)
            wait_all(sent)
            acc = dst[:, cols]
            for i in range(1, self.count):
                acc = acc + r2[e, h, i - 1].astype(F32)
            dst[:, cols] = acc

        def piece(self, high, h):
            n = self.size // PARTS
            start = (high * 2 + self.low) * self.size + h * n
            return pl.ds(pl.multiple_of(start, n), n)

        def gather(self, e, h, buf):
            g_s, g_r, f_s, f_r = self.gather_sems
            mine = buf.at[self.piece(self.high, h), :]
            copies = []
            for i in range(1, self.count):
                c = remote(mine, mine, g_s.at[e, h, i], g_r.at[e, h, i],
                           self.dev(((self.high + i) % self.count) * 2 + self.low))
                c.start()
                copies.append(c)
            c = remote(mine, mine, f_s.at[e, h, 0], f_r.at[e, h, 0], self.mate)
            c.start()
            return e, h, buf, copies, c

        def forward(self, states):
            g_s, g_r, f_s, f_r = self.gather_sems
            forwards = []
            for e, h, buf, copies, c0 in states:
                forwards.append(c0)
                for i in range(1, self.count):
                    copies[i - 1].wait_recv()
                    got = buf.at[self.piece((self.high + self.count - i) % self.count, h), :]
                    f = remote(got, got, f_s.at[e, h, i], f_r.at[e, h, i], self.mate)
                    f.start()
                    forwards.append(f)
            return states, forwards

        def complete(self, moves):
            states, forwards = moves
            for _, _, _, copies, _ in states:
                for c in copies:
                    c.wait_send()
            wait_all(forwards)

        def finish(self, states):
            self.complete(self.forward(states))

        def gather_all(self, e, buf):
            return [self.gather(e, h, buf) for h in range(PARTS)]

    def half(n, h):
        return pl.ds(h * (n // PARTS), n // PARTS)

    rowx = Axis(rows_n, row, on_row, chunk, (rs1, rr1, rs2, rr2),
                (rs1_s, rs1_r, rs2_s, rs2_r), (rg_s, rg_r, rf_s, rf_r))
    colx = Axis(cols_n, col, on_col, block, (cs1, cr1, cs2, cr2),
                (cs1_s, cs1_r, cs2_s, cs2_r), (cg_s, cg_r, cf_s, cf_r))

    my_rows = pl.ds(pl.multiple_of(col * block, block), block)
    tok_all[my_rows, :] = tokens[...]
    tok_state = colx.gather_all(0, tok_all)

    weights = (w_in, w_out)

    def times_left(k, vec):
        pieces_l[...] = pieces(vec)
        t = 768 if width % 768 == 0 else LANES

        def step(i, _):
            cs = pl.ds(pl.multiple_of(i * t, t), t)
            out = jnp.dot(pieces_l[...], weights[k][:, cs], preferred_element_type=F32)
            left[k, :, cs] = jnp.sum(out, axis=0, keepdims=True)
            return 0

        lax.fori_loop(0, width // t, step, 0)

    def times_right(k, vec):
        pieces_r[...] = pieces(vec)
        t = 768 if depth % 768 == 0 else LANES

        def step(i, _):
            rs = pl.ds(pl.multiple_of(i * t, t), t)
            out = lax.dot_general(
                pieces_r[...], weights[k][rs, :], (((1,), (1,)), ((), ())),
                preferred_element_type=F32,
            )
            right[k, :, rs] = jnp.sum(out, axis=0, keepdims=True)
            return 0

        lax.fori_loop(0, depth // t, step, 0)

    def matmul_nn(a, w, h):
        n = width // PARTS
        t = tile_of(n)

        def step(i, _):
            cs = pl.ds(pl.multiple_of(h * n + i * t, LANES), t)
            part[:, cs] = jnp.dot(a[...], w[:, cs], preferred_element_type=F32)
            return 0

        lax.fori_loop(0, n // t, step, 0)

    def matmul_nt(a, w, h):
        n = depth // PARTS
        t = tile_of(n)

        def step(i, _):
            cs = pl.ds(pl.multiple_of(h * n + i * t, LANES), t)
            outp[:, cs] = lax.dot_general(
                a[...], w[cs, :], (((1,), (1,)), ((), ())), preferred_element_type=F32
            )
            return 0

        lax.fori_loop(0, n // t, step, 0)

    def square_sum(vec):
        return jnp.sum(vec * vec, axis=1, keepdims=True)

    def send_left(it, k, squares):
        p_buf[it, k, row, :, :width] = left[k]
        p_buf[it, k, row, :, width:] = jnp.broadcast_to(squares, (1, LANES))
        return row_send(p_buf.at[it, k], p_s.at[it, k], p_r.at[it, k])

    def send_right(it, k, squares):
        q_buf[it, k, col, :, :depth] = right[k]
        q_buf[it, k, col, :, depth:] = jnp.broadcast_to(squares, (1, LANES))
        return col_send(q_buf.at[it, k], q_s.at[it, k], q_r.at[it, k])

    def right_half(it, k, copies):
        wait_all(copies)
        summed = slot_sum(p_buf.at[it, k], rows_n)
        vec = summed[:, :width]
        if it > 0:
            vec = vec / jnp.sqrt(summed[:, width : width + 1] + EPSILON)
        left[k] = vec
        times_right(k, vec)
        return send_right(it, k, square_sum(left[k]))

    def left_half(k, copies):
        wait_all(copies)
        summed = slot_sum(q_buf.at[0, k], cols_n)
        vec = summed[:, :depth] / jnp.sqrt(summed[:, depth : depth + 1] + EPSILON)
        times_left(k, vec)
        return send_left(1, k, square_sum(vec))

    def last_half(k, copies):
        wait_all(copies)
        summed = slot_sum(q_buf.at[1, k], cols_n)
        norm = jnp.sqrt(summed[:, depth : depth + 1] + EPSILON)
        v_units[k : k + 1, :] = left[k] / norm
        right[k] = summed[:, :depth] / norm
        n_buf[k, row] = jnp.broadcast_to(square_sum(right[k]), (1, LANES))
        return row_send(n_buf.at[k], n_s.at[k], n_r.at[k])

    def sigma_of(k, copies):
        wait_all(copies)
        sigma = jnp.sqrt(slot_sum(n_buf.at[k], rows_n)[:, 0:1] + EPSILON)
        u_next[k : k + 1, :] = right[k] / sigma
        return sigma, gains[k] / sigma

    zero = jnp.zeros((1, 1), F32)
    loads[0].wait()
    times_left(0, u_start[0:1, :])
    p0 = send_left(0, 0, zero)
    loads[1].wait()
    times_left(1, u_start[1:2, :])
    p1 = send_left(0, 1, zero)
    tok_moves = colx.forward(tok_state)
    q0 = right_half(0, 0, p0)
    colx.complete(tok_moves)
    matmul_nn(tok_all, w_in, 0)
    f0 = rowx.first(0, 0, part)
    q1 = right_half(0, 1, p1)
    p0 = left_half(0, q0)
    matmul_nn(tok_all, w_in, 1)
    f1 = rowx.first(0, 1, part)
    s0 = rowx.second(0, 0, part, hid, f0)
    p1 = left_half(1, q1)
    q0 = right_half(1, 0, p0)
    s1 = rowx.second(0, 1, part, hid, f1)
    q1 = right_half(1, 1, p1)
    n0 = last_half(0, q0)
    rowx.last(0, 0, hid, s0)
    rowx.last(0, 1, hid, s1)
    sigma_in, scale_in = sigma_of(0, n0)

    base = row * chunk

    def act_step(i, _):
        rs = pl.ds(pl.multiple_of(i * 16, 16), 16)
        h = hid[rs, :] * scale_in
        cdf = 0.5 * (1.0 + lax.erf(h * ROOT_HALF))
        slopes[rs, :] = cdf + h * jnp.exp(-0.5 * h * h) * INV_ROOT_TWO_PI
        act_all[pl.ds(pl.multiple_of(base + i * 16, 16), 16), :] = (h * cdf).astype(BF16)
        return 0

    steps = chunk // 16 // PARTS
    state = []
    for h in range(PARTS):
        lax.fori_loop(h * steps, (h + 1) * steps, act_step, 0)
        state.append(rowx.gather(0, h, act_all))
    n1 = last_half(1, q1)
    rowx.finish(state)

    matmul_nt(act_all, w_out, 0)
    f0 = colx.first(0, 0, outp)
    matmul_nt(act_all, w_out, 1)
    f1 = colx.first(0, 1, outp)
    sigma_out, scale_out = sigma_of(1, n1)
    s0 = colx.second(0, 0, outp, out_own, f0)
    s1 = colx.second(0, 1, outp, out_own, f1)
    colx.last(0, 0, out_own, s0)
    colx.last(0, 1, out_own, s1)
    loss_scale = 1.0 / jnp.sqrt(jnp.float32(total))
    g_all[my_rows, :] = (
        (scale_out * out_own[...] - target[...].astype(F32)) * loss_scale
    ).astype(BF16)
    colx.finish(colx.gather_all(1, g_all))

    matmul_nn(g_all, w_out, 0)
    f0 = rowx.first(1, 0, part)
    matmul_nn(g_all, w_out, 1)
    f1 = rowx.first(1, 1, part)
    s0 = rowx.second(1, 0, part, own, f0)
    s1 = rowx.second(1, 1, part, own, f1)
    rowx.last(1, 0, own, s0)
    rowx.last(1, 1, own, s1)

    def grad_step(i, sums):
        rs = pl.ds(pl.multiple_of(i * 16, 16), 16)
        ra = pl.ds(pl.multiple_of(base + i * 16, 16), 16)
        d = own[rs, :]
        grad = (scale_out * d * slopes[rs, :]).astype(BF16)
        gh_all[ra, :] = grad
        a = jnp.sum(grad.astype(F32) * hid[rs, :], axis=0, keepdims=True)
        b = jnp.sum(act_all[ra, :].astype(F32) * d, axis=0, keepdims=True)
        return sums[0] + a, sums[1] + b

    zeros = jnp.zeros((1, width), F32)
    sums = (zeros, zeros)
    state = []
    for h in range(PARTS):
        sums = lax.fori_loop(h * steps, (h + 1) * steps, grad_step, sums)
        state.append(rowx.gather(1, h, gh_all))
    sum_in, sum_out = sums
    tr_buf[row, 0:1] = jnp.broadcast_to(jnp.sum(sum_in, axis=1, keepdims=True), (1, LANES))
    tr_buf[row, 1:2] = jnp.broadcast_to(jnp.sum(sum_out, axis=1, keepdims=True), (1, LANES))
    tr_copies = row_send(tr_buf, tr_s, tr_r)
    rowx.finish(state)
    wait_all(tr_copies)
    tc_buf[col] = slot_sum(tr_buf, rows_n)
    tc_copies = col_send(tc_buf, tc_s, tc_r)

    matmul_nt(gh_all, w_in, 0)
    f0 = colx.first(1, 0, outp)
    matmul_nt(gh_all, w_in, 1)
    f1 = colx.first(1, 1, outp)
    s0 = colx.second(1, 0, outp, out_own, f0)
    s1 = colx.second(1, 1, outp, out_own, f1)
    wait_all(tc_copies)
    traces = slot_sum(tc_buf, cols_n)
    coeffs[0:1, :] = jnp.broadcast_to(scale_in, (1, LANES))
    coeffs[1:2, :] = jnp.broadcast_to(scale_out, (1, LANES))
    coeffs[2:3, :] = scale_in * traces[0:1] / sigma_in
    coeffs[3:4, :] = scale_out * traces[1:2] / sigma_out
    colx.last(1, 0, out_own, s0)
    colx.last(1, 1, out_own, s1)
    grad_tokens[...] = (scale_in * out_own[...]).astype(BF16)


def grads_body(tok, gh, g, act, u, v, coeffs, gin, gout):
    width = gh.shape[1]
    t = tile_of(width)
    for k, (a, b, out) in enumerate(((tok, gh, gin), (g, act, gout))):
        turned = jnp.transpose(a[...])
        shift = jnp.broadcast_to(u[k : k + 1, :] * coeffs[2 + k : 3 + k, 0:1], (LANES, u.shape[1]))
        shift = jnp.transpose(shift)[:, 0:1]
        scale = coeffs[k : k + 1, 0:1]
        for i in range(width // t):
            cs = slice(i * t, (i + 1) * t)
            prod = jnp.dot(turned, b[:, cs], preferred_element_type=F32)
            out[:, cs] = (scale * prod - shift * v[k : k + 1, cs]).astype(BF16)


def shards(rows_n, cols_n, tokens, target, w_in, w_out, gains, u_start):
    block, depth = tokens.shape
    width = w_in.shape[1]
    total = block * cols_n
    chunk = total // rows_n
    vmem = pl.BlockSpec(memory_space=pltpu.VMEM)
    dma = pltpu.SemaphoreType.DMA
    S = pltpu.VMEM
    ys, zs = rows_n // 2, cols_n // 2
    row_part = (2, PARTS, ys, chunk, width // PARTS)
    col_part = (2, PARTS, zs, block, depth // PARTS)
    tok_all, act_all, g_all, gh_all, u_next, v_units, coeffs, grad_tokens = pl.pallas_call(
        functools.partial(body, rows_n, cols_n),
        out_shape=(
            jax.ShapeDtypeStruct((total, depth), BF16),
            jax.ShapeDtypeStruct((total, width), BF16),
            jax.ShapeDtypeStruct((total, depth), BF16),
            jax.ShapeDtypeStruct((total, width), BF16),
            jax.ShapeDtypeStruct((2, depth), F32),
            jax.ShapeDtypeStruct((2, width), F32),
            jax.ShapeDtypeStruct((4, LANES), F32),
            jax.ShapeDtypeStruct((block, depth), BF16),
        ),
        in_specs=[vmem, vmem, pl.BlockSpec(memory_space=pltpu.SMEM), vmem]
        + [pl.BlockSpec(memory_space=pl.ANY)] * 2,
        out_specs=[vmem] * 8,
        scratch_shapes=[
            S((depth, width), BF16), S((depth, width), BF16),
            S((total, width), F32),
            S((chunk, width), F32), S((chunk, width), F32), S((chunk, width), F32),
            S(row_part, BF16), S(row_part, BF16), S(row_part, BF16), S(row_part, BF16),
            S((total, depth), F32), S((block, depth), F32),
            S(col_part, BF16), S(col_part, BF16), S(col_part, BF16), S(col_part, BF16),
            S((16, depth), BF16), S((16, width), BF16),
            S((2, 1, width), F32), S((2, 1, depth), F32),
            S((2, 2, rows_n, 1, width + LANES), F32),
            S((2, 2, cols_n, 1, depth + LANES), F32),
            S((2, rows_n, 1, LANES), F32), S((rows_n, 2, LANES), F32), S((cols_n, 2, LANES), F32),
            dma((2,)),
            dma((2, 2, rows_n)), dma((2, 2, rows_n)),
            dma((2, 2, cols_n)), dma((2, 2, cols_n)),
            dma((2, rows_n)), dma((2, rows_n)),
            dma((rows_n,)), dma((rows_n,)),
            dma((cols_n,)), dma((cols_n,)),
        ]
        + [dma((2, PARTS, ys))] * 4
        + [dma((2, PARTS, zs))] * 4
        + [dma((2, PARTS, ys))] * 4
        + [dma((2, PARTS, zs))] * 4,
        compiler_params=pltpu.CompilerParams(
            collective_id=0, has_side_effects=True, vmem_limit_bytes=58 * 1024 * 1024
        ),
    )(tokens, target, gains, u_start, w_in, w_out)
    rows = 256
    whole = lambda shape: pl.BlockSpec(shape, lambda i: (0, 0))
    side = lambda n: pl.BlockSpec((n, rows), lambda i: (0, i))
    grad_in, grad_out = pl.pallas_call(
        grads_body,
        grid=(depth // rows,),
        out_shape=(
            jax.ShapeDtypeStruct((depth, width), BF16),
            jax.ShapeDtypeStruct((depth, width), BF16),
        ),
        in_specs=[
            side(total), whole((total, width)), side(total), whole((total, width)),
            side(2), whole((2, width)), whole((4, LANES)),
        ],
        out_specs=[pl.BlockSpec((rows, width), lambda i: (i, 0))] * 2,
        compiler_params=pltpu.CompilerParams(vmem_limit_bytes=60 * 1024 * 1024),
    )(tok_all, gh_all, g_all, act_all, u_next, v_units, coeffs)
    return grad_tokens, grad_in, grad_out, u_next


def solution(mesh):
    placed = (
        P("col", "row"),
        P("col", "row"),
        P("row", "col"),
        P("row", "col"),
        P(),
        P(None, "row"),
    )
    return jax.shard_map(
        functools.partial(shards, mesh.shape["row"], mesh.shape["col"]),
        mesh=mesh,
        in_specs=placed,
        out_specs=(P("col", "row"), P("row", "col"), P("row", "col"), P(None, "row")),
        check_vma=False,
    )
```
